32 devices in a mesh: dp: 2 (over y), proto: 8 (over z, core), crop: 2 (over x).
Axes of the slice: x: 2, y: 2, z: 4, core: 2. Of those that a mesh axis runs over, the one named last changes fastest.
Arguments:
- embeddings: bfloat16 [256, 2, 4, 256], P(('dp', 'proto'), 'crop'), may hold values from -2 to 2
- codes: bfloat16 [256, 2, 65536], P('dp', 'crop', 'proto'), may hold values from 0 to 1, as said below
- prototypes: bfloat16 [8, 8192, 256], P('proto', ('dp', 'crop')), may hold values from -2 to 2
Outputs:
- grad_emb: float32 [256, 2, 4, 256], P(('dp', 'proto'), 'crop')
- grad_proto: float32 [8, 8192, 256], P('proto', ('dp', 'crop'))
The draws below stay inside these ranges and needn't reach their ends.
Inputs may be any that keep to these rules, and one draw needn't show every extreme that they name: `codes`: each image's code is a distribution over the prototypes: nonnegative entries that sum to about one over all 65536.
All inputs are finite; a program needn't handle non-finite values.
Results may differ from the reference program's by a relative error of at most 0.0031.
Values may be sent and summed in bfloat16 or wider, within the bound.
A program may use at most 64 MiB of HBM per device.

```python
import jax
import jax.numpy as jnp
from jax import lax

D = 256
K = 65536
GROUP = 4
BLOCKS = 8
KP = 8192
IMAGES = 256
N_DP = 2


def shared_direction(key):
    vector = jax.random.normal(jax.random.fold_in(key, 101), (D,), jnp.float32)
    return vector / jnp.sqrt(jnp.sum(vector * vector))


def draw_embeddings(key, part):
    direction = shared_direction(key)
    noise = jax.random.normal(jax.random.fold_in(key, 1), (IMAGES, 2, GROUP, D), jnp.float32) / jnp.sqrt(float(D))
    along = jax.random.uniform(jax.random.fold_in(key, 2), (IMAGES, 2, GROUP, 1), jnp.float32, 0.5, 1.5)
    scale = 0.3
    return jnp.clip(scale * (noise + along * direction), -2.0, 2.0).astype(jnp.bfloat16)


def draw_prototypes(key, part):
    direction = shared_direction(key)
    noise = jax.random.normal(jax.random.fold_in(key, 11), (BLOCKS, KP, D), jnp.float32) / jnp.sqrt(float(D))
    position = jnp.arange(BLOCKS * KP, dtype=jnp.float32).reshape(BLOCKS, KP, 1) / float(K)
    along = 0.35 * position
    scale = 0.25
    return jnp.clip(scale * (noise + along * direction), -2.0, 2.0).astype(jnp.bfloat16)


def draw_codes(key, part):
    logits = 2.5 * jax.random.normal(jax.random.fold_in(key, 22), (IMAGES, 2, K), jnp.float32)
    owner_rows = KP // (N_DP * 2)
    strip = jnp.arange(K, dtype=jnp.int32) % KP // owner_rows // 2
    image_block = jnp.arange(IMAGES, dtype=jnp.int32) // (IMAGES // N_DP)
    paired = (image_block + N_DP // 2) % N_DP
    bump = jnp.where(strip[None, :] == paired[:, None], 4.0, 0.0).astype(jnp.float32)
    return jax.nn.softmax(logits + bump[:, None, :], axis=-1).astype(jnp.bfloat16)


def setup_inputs(seed: int = 0) -> dict:
    key_of = jax.random.split(jax.random.key(seed), 4)
    embeddings = draw_embeddings(jax.random.fold_in(key_of[3], 71), 0)
    codes = draw_codes(jax.random.fold_in(key_of[3], 71), 0)
    prototypes = draw_prototypes(jax.random.fold_in(key_of[3], 71), 0)
    return dict(embeddings=embeddings, codes=codes, prototypes=prototypes)


sharpness_divisor = 0.1
epsilon = 1e-06

def reference(embeddings, codes, prototypes):
    floats = embeddings.astype(jnp.float32)
    emb_norm = jnp.sqrt(lax.optimization_barrier(jnp.sum(floats * floats, axis=-1, keepdims=True)) + epsilon)
    unit_emb = floats / emb_norm
    rounded = unit_emb.astype(jnp.bfloat16)
    proto_float = prototypes.astype(jnp.float32).reshape(K, D)
    proto_norm = jnp.sqrt(lax.optimization_barrier(jnp.sum(proto_float * proto_float, axis=-1, keepdims=True)) + epsilon)
    unit_proto = proto_float / proto_norm
    rescaled_input = unit_proto.astype(jnp.bfloat16)
    as_floats = rounded.astype(jnp.float32)
    local_sum = lax.optimization_barrier(jnp.sum(as_floats[:, :, 1:, :], axis=2))
    all_locals = local_sum[:, 0] + local_sum[:, 1]
    target_sums = jnp.stack([as_floats[:, 1, 0] + all_locals, as_floats[:, 0, 0] + all_locals], axis=1).astype(jnp.bfloat16)
    view_results = jnp.where(jnp.arange(GROUP) == 0, 1.0, 2.0).astype(jnp.float32)
    is_global = (jnp.arange(GROUP) == 0)[None, :, None]
    group_images = IMAGES // N_DP

    def one_group(running, dp_index):
        first_image = (dp_index * group_images).astype(jnp.int32)
        code_block = lax.dynamic_slice_in_dim(codes, first_image, group_images, 0)
        emb_block = lax.dynamic_slice_in_dim(rounded, first_image, group_images, 0)
        sum_block = lax.dynamic_slice_in_dim(target_sums, first_image, group_images, 0)
        code_terms = [jnp.dot(code_block[:, code_index], rescaled_input, preferred_element_type=jnp.float32) for code_index in (0, 1)]
        view_gradient_list = []
        for crop_group in range(2):
            view_row_list = emb_block[:, crop_group].reshape(group_images * GROUP, D)
            prototype_scores = jnp.dot(view_row_list, rescaled_input.T, preferred_element_type=jnp.float32) / sharpness_divisor
            exponent = jnp.exp(prototype_scores)
            probs = (exponent / lax.optimization_barrier(jnp.sum(exponent, axis=1, keepdims=True))).astype(jnp.bfloat16)
            softened_rows = jnp.dot(probs, rescaled_input, preferred_element_type=jnp.float32).reshape(group_images, GROUP, D)
            weighted = (view_row_list.astype(jnp.float32) * jnp.tile(view_results, group_images)[:, None]).astype(jnp.bfloat16)
            proto_term = jnp.dot(probs.T, weighted, preferred_element_type=jnp.float32)
            proto_term = proto_term - jnp.dot(code_block[:, crop_group].T, sum_block[:, crop_group], preferred_element_type=jnp.float32)
            running = running + proto_term
            partner = code_terms[1 - crop_group]
            both_terms = code_terms[0] + code_terms[1]
            goal_codes = jnp.where(is_global, partner[:, None, :], both_terms[:, None, :])
            view_gradient_list.append((softened_rows * view_results[None, :, None] - goal_codes) / sharpness_divisor)
        return (running, jnp.stack(view_gradient_list, axis=1))
    running, stacked = lax.scan(one_group, jnp.zeros((K, D), jnp.float32), jnp.arange(N_DP, dtype=jnp.int32))
    score_grad = stacked.reshape(IMAGES, 2, GROUP, D)
    grad_emb = (score_grad - unit_emb * lax.optimization_barrier(jnp.sum(unit_emb * score_grad, axis=-1, keepdims=True))) / emb_norm
    grad_proto = (running - unit_proto * lax.optimization_barrier(jnp.sum(unit_proto * running, axis=-1, keepdims=True))) / proto_norm
    return (grad_emb, grad_proto.reshape(BLOCKS, KP, D))
```

```python
import functools

import jax
import jax.numpy as jnp
from jax import lax
from jax.experimental import pallas as pl
from jax.experimental.pallas import tpu as pltpu
from jax.sharding import PartitionSpec as P

sharpness = 10.0
epsilon = 1e-06
MESH = pl.DeviceIdType.MESH


def unit_rows(values):
    floats = values.astype(jnp.float32)
    lengths = jnp.sqrt(jnp.sum(floats * floats, axis=-1, keepdims=True) + epsilon)
    return floats / lengths, lengths


def kernel(
    sizes,
    emb_ref,
    codes_ref,
    proto_ref,
    gemb_ref,
    gproto_ref,
    z_all,
    c_all,
    c_buf,
    ct_buf,
    e_all,
    tot_buf,
    tot_in1,
    tot_mid,
    tot_in2,
    rc_buf,
    cp_buf,
    ts_buf,
    rs1_in,
    rs2_out,
    rs2_in,
    rs3_out,
    rs3_in,
    s1_send,
    s1_recv,
    s2_send,
    s2_recv,
    s3_send,
    s3_recv,
    code_send,
    code_recv,
    code_local,
    t1_send,
    t1_recv,
    t2_send,
    t2_recv,
    r1_send,
    r1_recv,
    r2_send,
    r2_recv,
    r3_send,
    r3_recv,
):
    n_dp, n_proto, n_crop, images, crops, tile = sizes
    n_plane, n_z = n_dp * n_crop, n_proto // 2
    shard = images * crops
    unit = n_z * shard
    group = n_proto * images
    owned = proto_ref.shape[0]
    tiles = owned // tile

    my_dp, my_proto, my_crop = (lax.axis_index(a) for a in ("dp", "proto", "crop"))
    plane = my_dp * n_crop + my_crop
    zi, core = my_proto // 2, my_proto % 2
    sibling = {"proto": zi * 2 + (1 - core)}

    def plane_peer(d):
        q = lax.rem(plane + d, n_plane)
        return q, {"dp": q // n_crop, "crop": q % n_crop}

    def plane_from(d):
        return lax.rem(plane + n_plane - d, n_plane)

    def z_peer(d):
        other = lax.rem(zi + d, n_z)
        return other, {"proto": other * 2 + core}

    def proto_peer(d):
        return {"proto": lax.rem(my_proto + d, n_proto)}

    def remote(src, dst, send, recv, device):
        return pltpu.make_async_remote_copy(
            src_ref=src, dst_ref=dst, send_sem=send, recv_sem=recv,
            device_id=device, device_id_type=MESH,
        )

    barrier = pltpu.get_barrier_semaphore()
    for d in range(1, n_proto):
        pl.semaphore_signal(barrier, inc=1, device_id=proto_peer(d), device_id_type=MESH)
    for d in range(1, n_plane):
        pl.semaphore_signal(barrier, inc=1, device_id=plane_peer(d)[1], device_id_type=MESH)

    own_codes = pltpu.make_async_copy(
        codes_ref.at[:, pl.ds(pl.multiple_of(plane * owned, owned), owned)],
        c_all.at[pl.ds(pl.multiple_of(plane * group, group), group), :],
        code_local,
    )
    own_codes.start()
    own_rows = pl.ds(pl.multiple_of(zi * shard, shard), shard)
    z_all[core, plane, own_rows, :] = unit_rows(emb_ref[...])[0].astype(jnp.bfloat16)

    pl.semaphore_wait(barrier, n_proto - 1 + n_plane - 1)

    sent = []
    s1 = []
    for d in range(1, n_z):
        ref = z_all.at[core, plane, own_rows, :]
        s1.append(remote(ref, ref, s1_send.at[d - 1], s1_recv.at[d - 1], z_peer(d)[1]))
        s1[-1].start()

    def tile_rows(t):
        return pl.ds(pl.multiple_of(t * tile, tile), tile)

    def normalize_tile(t, carry):
        unit_w = unit_rows(proto_ref[tile_rows(t), :])[0]
        c_buf[tile_rows(t), :] = unit_w.astype(jnp.bfloat16)
        ct_buf[:, tile_rows(t)] = unit_w.T.astype(jnp.bfloat16)
        return carry

    lax.fori_loop(0, tiles, normalize_tile, 0)

    for copy in s1:
        copy.wait_recv()
    s2 = []
    for d in range(1, n_plane):
        ref = z_all.at[core, plane]
        s2.append(remote(ref, ref, s2_send.at[d - 1], s2_recv.at[d - 1], plane_peer(d)[1]))
        s2[-1].start()
    code_copies = []
    for d in range(1, n_plane):
        q, device = plane_peer(d)
        code_copies.append(remote(
            codes_ref.at[:, pl.ds(pl.multiple_of(q * owned, owned), owned)],
            c_all.at[pl.ds(pl.multiple_of(plane * group, group), group), :],
            code_send.at[d - 1], code_recv.at[d - 1], device,
        ))
        code_copies[-1].start()
    sent += code_copies

    def score_unit(half, q):
        rows = z_all[half, q]

        def score_tile(t, sums):
            scores = lax.dot_general(
                c_buf[tile_rows(t), :], rows, (((1,), (1,)), ((), ())),
                preferred_element_type=jnp.float32,
            )
            exponent = jnp.exp(scores * sharpness)
            e_all[half * n_plane + q, tile_rows(t), :] = exponent.astype(jnp.bfloat16)
            return sums + jnp.sum(exponent, axis=0, keepdims=True)

        sums = lax.fori_loop(0, tiles, score_tile, jnp.zeros((1, unit), jnp.float32))
        tot_buf[pl.ds(half * n_plane + q, 1), :] = sums

    s3 = []
    for d in range(n_plane):
        q = plane_from(d)
        if d:
            s2[d - 1].wait_recv()
        ref = z_all.at[core, q]
        s3.append(remote(ref, ref, s3_send.at[d], s3_recv.at[d], sibling))
        s3[-1].start()
        score_unit(core, q)
    for d in range(n_plane):
        s3[d].wait_recv()
        score_unit(1 - core, plane_from(d))

    t1 = []
    for d in range(1, n_proto):
        t1.append(remote(
            tot_buf, tot_in1.at[d - 1], t1_send.at[d - 1], t1_recv.at[d - 1], proto_peer(d)
        ))
        t1[-1].start()

    def soften_unit(u, carry):
        columns = jnp.dot(ct_buf[...], e_all[u], preferred_element_type=jnp.float32)
        rc_buf[u] = columns.T
        return carry

    lax.fori_loop(0, 2 * n_plane, soften_unit, 0)

    total = tot_buf[...]
    for d in range(1, n_proto):
        t1[d - 1].wait_recv()
        total = total + tot_in1[d - 1]
    tot_mid[...] = total
    t2 = []
    for d in range(1, n_plane):
        t2.append(remote(
            tot_mid, tot_in2.at[d - 1], t2_send.at[d - 1], t2_recv.at[d - 1], plane_peer(d)[1]
        ))
        t2[-1].start()
    sent += t2

    def image_rows(half, z):
        return pl.ds((z * 2 + half) * images, images)

    def crop_rows(z, v):
        return pl.ds(z * shard + v * images, images)

    def target_group(a, carry):
        for half in range(2):
            for z in range(n_z):
                locals_sum = None
                for g in range(n_crop):
                    for v in range(1, crops):
                        term = z_all[half, a * n_crop + g, crop_rows(z, v), :].astype(jnp.float32)
                        locals_sum = term if locals_sum is None else locals_sum + term
                for t in range(n_crop):
                    other = z_all[half, a * n_crop + 1 - t, crop_rows(z, 0), :]
                    ts_buf[a, t, image_rows(half, z), :] = (
                        locals_sum + other.astype(jnp.float32)
                    ).astype(jnp.bfloat16)
        return carry

    lax.fori_loop(0, n_dp, target_group, 0)

    own_codes.wait()
    for copy in code_copies:
        copy.wait_recv()

    def code_products(q, carry):
        rows = pl.ds(pl.multiple_of(q * group, group), group)
        cp_buf[q] = jnp.dot(c_all[rows, :], c_buf[...], preferred_element_type=jnp.float32)
        return carry

    lax.fori_loop(0, n_plane, code_products, 0)

    total = tot_mid[...]
    for d in range(1, n_plane):
        t2[d - 1].wait_recv()
        total = total + tot_in2[d - 1]
    crop_of = lax.rem(lax.broadcasted_iota(jnp.int32, total.shape, 1) // images, crops)
    tot_buf_weights = jnp.where(crop_of == 0, 1.0, 2.0) / total
    for copy in t1 + s1 + s2 + s3:
        copy.wait_send()
    tot_buf[...] = tot_buf_weights

    lanes = 128

    def row_unit(half, q):
        u = half * n_plane + q
        weights = tot_buf[pl.ds(u, 1), :]
        a, g = q // n_crop, q % n_crop
        for b in range(unit // lanes):
            part = pl.ds(b * lanes, lanes)
            column = jnp.broadcast_to(weights[:, b * lanes:(b + 1) * lanes], (lanes, lanes)).T
            column = jnp.concatenate([column] * (z_all.shape[-1] // lanes), axis=1)
            z_all[half, q, part, :] = (
                z_all[half, q, part, :].astype(jnp.float32) * column
            ).astype(jnp.bfloat16)
            rc_buf[u, part, :] = rc_buf[u, part, :] * column
        for z in range(n_z):
            rows = pl.ds(pl.multiple_of((z * 2 + half) * images, images), images)
            other = cp_buf[a * n_crop + 1 - g, rows, :]
            both = other + cp_buf[q, rows, :]
            for v in range(crops):
                code_term = other if v == 0 else both
                rc_buf[u, crop_rows(z, v), :] = (
                    rc_buf[u, crop_rows(z, v), :] - code_term
                ) * sharpness

    r1 = []
    for d in range(n_plane):
        q = plane_from(d)
        row_unit(1 - core, q)
        r1.append(remote(
            rc_buf.at[(1 - core) * n_plane + q], rs1_in.at[q],
            r1_send.at[d], r1_recv.at[d], sibling,
        ))
        r1[-1].start()
    sent += r1
    for d in range(n_plane):
        row_unit(core, plane_from(d))

    r2 = []
    for d in range(n_plane):
        r1[d].wait_recv()
        q = plane_from(d)
        if d == 0:
            continue
        rs2_out[d - 1] = (rc_buf[core * n_plane + q] + rs1_in[q]).astype(jnp.bfloat16)
        device = {"dp": q // n_crop, "crop": q % n_crop}
        r2.append(remote(
            rs2_out.at[d - 1], rs2_in.at[d - 1], r2_send.at[d - 1], r2_recv.at[d - 1], device
        ))
        r2[-1].start()
    sent += r2

    def proto_tile(t, carry):
        rows = tile_rows(t)
        grad = jnp.dot(e_all[0, rows, :], z_all[0, 0], preferred_element_type=jnp.float32)
        for u in range(1, 2 * n_plane):
            grad = grad + jnp.dot(
                e_all[u, rows, :], z_all[u // n_plane, u % n_plane], preferred_element_type=jnp.float32
            )
        targets = ts_buf[...].reshape(n_plane * group, ts_buf.shape[-1])
        grad = grad - lax.dot_general(
            c_all[:, rows], targets, (((0,), (0,)), ((), ())), preferred_element_type=jnp.float32
        )
        unit_w, length = unit_rows(proto_ref[rows, :])
        along = jnp.sum(unit_w * grad, axis=-1, keepdims=True)
        gproto_ref[rows, :] = (grad - unit_w * along) / length
        return carry

    first = tiles // 2
    lax.fori_loop(0, first, proto_tile, 0)

    rows_sum = rc_buf[core * n_plane + plane] + rs1_in[plane]
    for copy in r2:
        copy.wait_recv()
    for d in range(1, n_plane):
        rows_sum = rows_sum + rs2_in[d - 1].astype(jnp.float32)
    rs3_out[...] = rows_sum
    r3 = []
    for d in range(1, n_z):
        other, device = z_peer(d)
        r3.append(remote(
            rs3_out.at[pl.ds(pl.multiple_of(other * shard, shard), shard), :], rs3_in.at[d - 1],
            r3_send.at[d - 1], r3_recv.at[d - 1], device,
        ))
        r3[-1].start()
    sent += r3

    lax.fori_loop(first, tiles, proto_tile, 0)

    score_grad = rs3_out[own_rows, :]
    for d in range(1, n_z):
        r3[d - 1].wait_recv()
        score_grad = score_grad + rs3_in[d - 1]
    unit_e, length = unit_rows(emb_ref[...])
    along = jnp.sum(unit_e * score_grad, axis=-1, keepdims=True)
    gemb_ref[...] = (score_grad - unit_e * along) / length
    for copy in sent:
        copy.wait_send()


def on_device(sizes, embeddings, codes, prototypes):
    n_dp, n_proto, n_crop = sizes
    images, _, crops, features = embeddings.shape
    owned = prototypes.shape[1]
    n_plane, n_z = n_dp * n_crop, n_proto // 2
    shard = images * crops
    unit = n_z * shard
    group = codes.shape[0]
    units = 2 * n_plane
    tile = min(owned, 256)
    rows = embeddings[:, 0].transpose(1, 0, 2).reshape(shard, features)
    vmem = pl.BlockSpec(memory_space=pltpu.VMEM)
    dma = pltpu.SemaphoreType.DMA
    bf16, f32 = jnp.bfloat16, jnp.float32
    pairs = [n_z - 1, n_plane - 1, n_plane, n_plane - 1]
    sems = []
    for count in pairs:
        sems += [dma((max(count, 1),)), dma((max(count, 1),))]
    sems.append(dma)
    for count in (n_proto - 1, n_plane - 1, n_plane, n_plane - 1, n_z - 1):
        sems += [dma((max(count, 1),)), dma((max(count, 1),))]
    grad_emb, grad_proto = pl.pallas_call(
        functools.partial(kernel, (n_dp, n_proto, n_crop, images, crops, tile)),
        out_shape=(
            jax.ShapeDtypeStruct((shard, features), f32),
            jax.ShapeDtypeStruct((owned, features), f32),
        ),
        in_specs=[vmem, pl.BlockSpec(memory_space=pl.ANY), vmem],
        out_specs=(vmem, vmem),
        scratch_shapes=[
            pltpu.VMEM((2, n_plane, unit, features), bf16),
            pltpu.VMEM((n_plane * group, owned), bf16),
            pltpu.VMEM((owned, features), bf16),
            pltpu.VMEM((features, owned), bf16),
            pltpu.VMEM((units, owned, unit), bf16),
            pltpu.VMEM((units, unit), f32),
            pltpu.VMEM((n_proto - 1, units, unit), f32),
            pltpu.VMEM((units, unit), f32),
            pltpu.VMEM((max(n_plane - 1, 1), units, unit), f32),
            pltpu.VMEM((units, unit, features), f32),
            pltpu.VMEM((n_plane, group, features), f32),
            pltpu.VMEM((n_dp, n_crop, group, features), bf16),
            pltpu.VMEM((n_plane, unit, features), f32),
            pltpu.VMEM((max(n_plane - 1, 1), unit, features), bf16),
            pltpu.VMEM((max(n_plane - 1, 1), unit, features), bf16),
            pltpu.VMEM((unit, features), f32),
            pltpu.VMEM((max(n_z - 1, 1), shard, features), f32),
        ] + sems,
        compiler_params=pltpu.CompilerParams(
            collective_id=0, has_side_effects=True, vmem_limit_bytes=62 * 2**20
        ),
        cost_estimate=pl.CostEstimate(
            flops=6 * units * unit * owned * features, bytes_accessed=8 * owned * features,
            transcendentals=units * unit * owned,
        ),
    )(rows, codes[:, 0], prototypes[0])
    grad_emb = grad_emb.reshape(crops, images, features).transpose(1, 0, 2)
    return grad_emb[:, None], grad_proto[None]


def solution(mesh):
    sizes = tuple(mesh.shape[a] for a in ("dp", "proto", "crop"))
    return jax.shard_map(
        functools.partial(on_device, sizes),
        mesh=mesh,
        in_specs=(
            P(("dp", "proto"), "crop", None, None),
            P("dp", "crop", "proto"),
            P("proto", ("dp", "crop"), None),
        ),
        out_specs=(P(("dp", "proto"), "crop", None, None), P("proto", ("dp", "crop"), None)),
        check_vma=False,
    )
```

```python
import functools

import jax
import jax.numpy as jnp
from jax import lax
from jax.experimental import pallas as pl
from jax.experimental.pallas import tpu as pltpu
from jax.sharding import PartitionSpec as P

sharpness = 10.0
epsilon = 1e-06
MESH = pl.DeviceIdType.MESH


def unit_rows(values):
    floats = values.astype(jnp.float32)
    lengths = jnp.sqrt(jnp.sum(floats * floats, axis=-1, keepdims=True) + epsilon)
    return floats / lengths, lengths


def kernel(
    sizes,
    emb_ref,
    codes_ref,
    proto_ref,
    gemb_ref,
    gproto_ref,
    z_all,
    c_all,
    c_buf,
    ct_buf,
    e_all,
    tot_buf,
    tot_in1,
    tot_mid,
    tot_in2,
    rc_buf,
    cp_buf,
    ts_buf,
    rs1_in,
    rs2_out,
    rs2_in,
    rs3_out,
    rs3_in,
    s1_send,
    s1_recv,
    s2_send,
    s2_recv,
    s3_send,
    s3_recv,
    code_send,
    code_recv,
    code_local,
    t1_send,
    t1_recv,
    t2_send,
    t2_recv,
    r1_send,
    r1_recv,
    r2_send,
    r2_recv,
    r3_send,
    r3_recv,
):
    n_dp, n_proto, n_crop, images, crops, tile = sizes
    n_plane, n_z = n_dp * n_crop, n_proto // 2
    shard = images * crops
    unit = n_z * shard
    group = n_proto * images
    owned = proto_ref.shape[0]
    tiles = owned // tile

    my_dp, my_proto, my_crop = (lax.axis_index(a) for a in ("dp", "proto", "crop"))
    plane = my_dp * n_crop + my_crop
    zi, core = my_proto // 2, my_proto % 2
    sibling = {"proto": zi * 2 + (1 - core)}

    def plane_peer(d):
        q = lax.rem(plane + d, n_plane)
        return q, {"dp": q // n_crop, "crop": q % n_crop}

    def plane_from(d):
        return lax.rem(plane + n_plane - d, n_plane)

    def z_peer(d):
        other = lax.rem(zi + d, n_z)
        return other, {"proto": other * 2 + core}

    def proto_peer(d):
        return {"proto": lax.rem(my_proto + d, n_proto)}

    def remote(src, dst, send, recv, device):
        return pltpu.make_async_remote_copy(
            src_ref=src, dst_ref=dst, send_sem=send, recv_sem=recv,
            device_id=device, device_id_type=MESH,
        )

    barrier = pltpu.get_barrier_semaphore()
    for d in range(1, n_proto):
        pl.semaphore_signal(barrier, inc=1, device_id=proto_peer(d), device_id_type=MESH)
    for d in range(1, n_plane):
        pl.semaphore_signal(barrier, inc=1, device_id=plane_peer(d)[1], device_id_type=MESH)

    own_codes = pltpu.make_async_copy(
        codes_ref.at[:, pl.ds(pl.multiple_of(plane * owned, owned), owned)],
        c_all.at[pl.ds(pl.multiple_of(plane * group, group), group), :],
        code_local,
    )
    own_codes.start()
    emb_floats = emb_ref[...].astype(jnp.float32)
    emb_rows = jnp.concatenate([emb_floats[:, v, :] for v in range(crops)], axis=0)
    unit_e, emb_length = unit_rows(emb_rows)
    own_rows = pl.ds(pl.multiple_of(zi * shard, shard), shard)
    z_all[core, plane, own_rows, :] = unit_e.astype(jnp.bfloat16)

    pl.semaphore_wait(barrier, n_proto - 1 + n_plane - 1)

    sent = []
    s1 = []
    for d in range(1, n_z):
        ref = z_all.at[core, plane, own_rows, :]
        s1.append(remote(ref, ref, s1_send.at[d - 1], s1_recv.at[d - 1], z_peer(d)[1]))
        s1[-1].start()

    s2 = {}

    def send_shard(dz):
        source = lax.rem(zi + n_z - dz, n_z)
        ref = z_all.at[core, plane, pl.ds(pl.multiple_of(source * shard, shard), shard), :]
        for d in range(1, n_plane):
            sem = dz * (n_plane - 1) + d - 1
            s2[dz, d] = remote(ref, ref, s2_send.at[sem], s2_recv.at[sem], plane_peer(d)[1])
            s2[dz, d].start()

    send_shard(0)

    def tile_rows(t):
        return pl.ds(pl.multiple_of(t * tile, tile), tile)

    def normalize_tile(t, carry):
        unit_w = unit_rows(proto_ref[tile_rows(t), :])[0]
        c_buf[tile_rows(t), :] = unit_w.astype(jnp.bfloat16)
        ct_buf[:, tile_rows(t)] = unit_w.T.astype(jnp.bfloat16)
        return carry

    lax.fori_loop(0, tiles, normalize_tile, 0, unroll=True)

    for dz in range(1, n_z):
        s1[dz - 1].wait_recv()
        send_shard(dz)
    code_copies = []
    for d in range(1, n_plane):
        q, device = plane_peer(d)
        code_copies.append(remote(
            codes_ref.at[:, pl.ds(pl.multiple_of(q * owned, owned), owned)],
            c_all.at[pl.ds(pl.multiple_of(plane * group, group), group), :],
            code_send.at[d - 1], code_recv.at[d - 1], device,
        ))
        code_copies[-1].start()
    sent += code_copies

    def score_unit(half, q):
        rows = z_all[half, q]

        def score_tile(t, sums):
            scores = lax.dot_general(
                c_buf[tile_rows(t), :], rows, (((1,), (1,)), ((), ())),
                preferred_element_type=jnp.float32,
            )
            exponent = jnp.exp(scores * sharpness)
            e_all[half * n_plane + q, tile_rows(t), :] = exponent.astype(jnp.bfloat16)
            return sums + jnp.sum(exponent, axis=0, keepdims=True)

        sums = lax.fori_loop(
            0, tiles, score_tile, jnp.zeros((1, unit), jnp.float32), unroll=True
        )
        tot_buf[pl.ds(half * n_plane + q, 1), :] = sums

    def soften_unit(u):
        columns = jnp.dot(ct_buf[...], e_all[u], preferred_element_type=jnp.float32)
        rc_buf[u] = columns.T

    s3 = []
    for d in range(n_plane):
        q = plane_from(d)
        for dz in range(n_z if d else 0):
            s2[dz, d].wait_recv()
        ref = z_all.at[core, q]
        s3.append(remote(ref, ref, s3_send.at[d], s3_recv.at[d], sibling))
        s3[-1].start()
        score_unit(core, q)
        soften_unit(core * n_plane + q)
    for d in range(n_plane):
        s3[d].wait_recv()
        score_unit(1 - core, plane_from(d))

    t1 = []
    for d in range(1, n_proto):
        t1.append(remote(
            tot_buf, tot_in1.at[d - 1], t1_send.at[d - 1], t1_recv.at[d - 1], proto_peer(d)
        ))
        t1[-1].start()

    for d in range(n_plane):
        soften_unit((1 - core) * n_plane + plane_from(d))

    total = tot_buf[...]
    for d in range(1, n_proto):
        t1[d - 1].wait_recv()
        total = total + tot_in1[d - 1]
    tot_mid[...] = total
    t2 = []
    for d in range(1, n_plane):
        t2.append(remote(
            tot_mid, tot_in2.at[d - 1], t2_send.at[d - 1], t2_recv.at[d - 1], plane_peer(d)[1]
        ))
        t2[-1].start()
    sent += t2

    def image_rows(half, z):
        return pl.ds((z * 2 + half) * images, images)

    def crop_rows(z, v):
        return pl.ds(z * shard + v * images, images)

    def target_group(a, carry):
        for half in range(2):
            for z in range(n_z):
                locals_sum = None
                for g in range(n_crop):
                    for v in range(1, crops):
                        term = z_all[half, a * n_crop + g, crop_rows(z, v), :].astype(jnp.float32)
                        locals_sum = term if locals_sum is None else locals_sum + term
                for t in range(n_crop):
                    other = z_all[half, a * n_crop + 1 - t, crop_rows(z, 0), :]
                    ts_buf[a, t, image_rows(half, z), :] = (
                        locals_sum + other.astype(jnp.float32)
                    ).astype(jnp.bfloat16)
        return carry

    lax.fori_loop(0, n_dp, target_group, 0)

    own_codes.wait()
    for copy in code_copies:
        copy.wait_recv()

    code_rows = n_plane * group
    chunk = min(code_rows, 512)

    def code_products(k, carry):
        rows = pl.ds(pl.multiple_of(k * chunk, chunk), chunk)
        cp_buf[rows, :] = jnp.dot(
            c_all[rows, :], c_buf[...], preferred_element_type=jnp.float32
        )
        return carry

    lax.fori_loop(0, code_rows // chunk, code_products, 0)

    total = tot_mid[...]
    for d in range(1, n_plane):
        t2[d - 1].wait_recv()
        total = total + tot_in2[d - 1]
    crop_of = lax.rem(lax.broadcasted_iota(jnp.int32, total.shape, 1) // images, crops)
    tot_buf_weights = jnp.where(crop_of == 0, 1.0, 2.0) / total
    for copy in t1 + s1 + list(s2.values()) + s3:
        copy.wait_send()
    tot_buf[...] = tot_buf_weights

    lanes = 128

    def row_unit(half, q):
        u = half * n_plane + q
        weights = tot_buf[pl.ds(u, 1), :]
        a, g = q // n_crop, q % n_crop
        for b in range(unit // lanes):
            part = pl.ds(b * lanes, lanes)
            column = jnp.broadcast_to(weights[:, b * lanes:(b + 1) * lanes], (lanes, lanes)).T
            column = jnp.concatenate([column] * (z_all.shape[-1] // lanes), axis=1)
            z_all[half, q, part, :] = (
                z_all[half, q, part, :].astype(jnp.float32) * column
            ).astype(jnp.bfloat16)
            rc_buf[u, part, :] = rc_buf[u, part, :] * column
        for z in range(n_z):
            def code_part(t):
                start = (a * n_crop + t) * group + (z * 2 + half) * images
                return cp_buf[pl.ds(pl.multiple_of(start, images), images), :]

            other = code_part(1 - g)
            both = other + code_part(g)
            for v in range(crops):
                code_term = other if v == 0 else both
                rc_buf[u, crop_rows(z, v), :] = (
                    rc_buf[u, crop_rows(z, v), :] - code_term
                ) * sharpness

    r1 = {}
    order = list(range(1, n_plane)) + [0]
    for d in order:
        q = plane_from(d)
        row_unit(1 - core, q)
        r1[d] = remote(
            rc_buf.at[(1 - core) * n_plane + q], rs1_in.at[q],
            r1_send.at[d], r1_recv.at[d], sibling,
        )
        r1[d].start()
    sent += list(r1.values())

    r2 = []
    for d in order:
        q = plane_from(d)
        row_unit(core, q)
        r1[d].wait_recv()
        if d == 0:
            continue
        rs2_out[d - 1] = (rc_buf[core * n_plane + q] + rs1_in[q]).astype(jnp.bfloat16)
        device = {"dp": q // n_crop, "crop": q % n_crop}
        r2.append(remote(
            rs2_out.at[d - 1], rs2_in.at[d - 1], r2_send.at[d - 1], r2_recv.at[d - 1], device
        ))
        r2[-1].start()
    sent += r2

    wide = min(owned, 2 * tile)

    def proto_tile(t, carry):
        rows = pl.ds(pl.multiple_of(t * wide, wide), wide)
        exponents = jnp.concatenate([e_all[u, rows, :] for u in range(2 * n_plane)], axis=1)
        weighted = z_all[...].reshape(2 * n_plane * unit, z_all.shape[-1])
        grad = jnp.dot(exponents, weighted, preferred_element_type=jnp.float32)
        targets = ts_buf[...].reshape(n_plane * group, ts_buf.shape[-1])
        grad = grad - lax.dot_general(
            c_all[:, rows], targets, (((0,), (0,)), ((), ())), preferred_element_type=jnp.float32
        )
        unit_w, length = unit_rows(proto_ref[rows, :])
        along = jnp.sum(unit_w * grad, axis=-1, keepdims=True)
        gproto_ref[rows, :] = (grad - unit_w * along) / length
        return carry

    first = (owned // wide) * 3 // 4
    lax.fori_loop(0, first, proto_tile, 0)

    rows_sum = rc_buf[core * n_plane + plane] + rs1_in[plane]
    for copy in r2:
        copy.wait_recv()
    for d in range(1, n_plane):
        rows_sum = rows_sum + rs2_in[d - 1].astype(jnp.float32)
    rs3_out[...] = rows_sum
    r3 = []
    for d in range(1, n_z):
        other, device = z_peer(d)
        r3.append(remote(
            rs3_out.at[pl.ds(pl.multiple_of(other * shard, shard), shard), :], rs3_in.at[d - 1],
            r3_send.at[d - 1], r3_recv.at[d - 1], device,
        ))
        r3[-1].start()
    sent += r3

    lax.fori_loop(first, owned // wide, proto_tile, 0)

    score_grad = rs3_out[own_rows, :]
    for d in range(1, n_z):
        r3[d - 1].wait_recv()
        score_grad = score_grad + rs3_in[d - 1]
    along = jnp.sum(unit_e * score_grad, axis=-1, keepdims=True)
    grad_rows = (score_grad - unit_e * along) / emb_length
    for v in range(crops):
        gemb_ref[:, v, :] = grad_rows[v * images:(v + 1) * images]
    for copy in sent:
        copy.wait_send()


def on_device(sizes, embeddings, codes, prototypes):
    n_dp, n_proto, n_crop = sizes
    images, _, crops, features = embeddings.shape
    owned = prototypes.shape[1]
    n_plane, n_z = n_dp * n_crop, n_proto // 2
    shard = images * crops
    unit = n_z * shard
    group = codes.shape[0]
    units = 2 * n_plane
    tile = min(owned, 256)
    vmem = pl.BlockSpec(memory_space=pltpu.VMEM)
    dma = pltpu.SemaphoreType.DMA
    bf16, f32 = jnp.bfloat16, jnp.float32
    pairs = [n_z - 1, n_z * (n_plane - 1), n_plane, n_plane - 1]
    sems = []
    for count in pairs:
        sems += [dma((max(count, 1),)), dma((max(count, 1),))]
    sems.append(dma)
    for count in (n_proto - 1, n_plane - 1, n_plane, n_plane - 1, n_z - 1):
        sems += [dma((max(count, 1),)), dma((max(count, 1),))]
    grad_emb, grad_proto = pl.pallas_call(
        functools.partial(kernel, (n_dp, n_proto, n_crop, images, crops, tile)),
        out_shape=(
            jax.ShapeDtypeStruct((images, crops, features), f32),
            jax.ShapeDtypeStruct((owned, features), f32),
        ),
        in_specs=[vmem, pl.BlockSpec(memory_space=pl.ANY), vmem],
        out_specs=(vmem, vmem),
        scratch_shapes=[
            pltpu.VMEM((2, n_plane, unit, features), bf16),
            pltpu.VMEM((n_plane * group, owned), bf16),
            pltpu.VMEM((owned, features), bf16),
            pltpu.VMEM((features, owned), bf16),
            pltpu.VMEM((units, owned, unit), bf16),
            pltpu.VMEM((units, unit), f32),
            pltpu.VMEM((n_proto - 1, units, unit), f32),
            pltpu.VMEM((units, unit), f32),
            pltpu.VMEM((max(n_plane - 1, 1), units, unit), f32),
            pltpu.VMEM((units, unit, features), f32),
            pltpu.VMEM((n_plane * group, features), f32),
            pltpu.VMEM((n_dp, n_crop, group, features), bf16),
            pltpu.VMEM((n_plane, unit, features), f32),
            pltpu.VMEM((max(n_plane - 1, 1), unit, features), bf16),
            pltpu.VMEM((max(n_plane - 1, 1), unit, features), bf16),
            pltpu.VMEM((unit, features), f32),
            pltpu.VMEM((max(n_z - 1, 1), shard, features), f32),
        ] + sems,
        compiler_params=pltpu.CompilerParams(
            collective_id=0, has_side_effects=True, vmem_limit_bytes=62 * 2**20
        ),
        cost_estimate=pl.CostEstimate(
            flops=6 * units * unit * owned * features, bytes_accessed=8 * owned * features,
            transcendentals=units * unit * owned,
        ),
    )(embeddings[:, 0], codes[:, 0], prototypes[0])
    return grad_emb[:, None], grad_proto[None]


def solution(mesh):
    sizes = tuple(mesh.shape[a] for a in ("dp", "proto", "crop"))
    return jax.shard_map(
        functools.partial(on_device, sizes),
        mesh=mesh,
        in_specs=(
            P(("dp", "proto"), "crop", None, None),
            P("dp", "crop", "proto"),
            P("proto", ("dp", "crop"), None),
        ),
        out_specs=(P(("dp", "proto"), "crop", None, None), P("proto", ("dp", "crop"), None)),
        check_vma=False,
    )
```

```python
import functools
import math

import jax
import jax.numpy as jnp
from jax import lax
from jax.experimental import pallas as pl
from jax.experimental.pallas import tpu as pltpu
from jax.sharding import PartitionSpec as P

sharpness = 10.0
epsilon = 1e-06
MESH = pl.DeviceIdType.MESH


def unit_rows(values):
    floats = values.astype(jnp.float32)
    lengths = jnp.sqrt(jnp.sum(floats * floats, axis=-1, keepdims=True) + epsilon)
    return floats / lengths, lengths


def kernel(
    sizes,
    emb_ref,
    codes_ref,
    proto_ref,
    gemb_ref,
    gproto_ref,
    gp_buf,
    gp_sem,
    z_all,
    c_all,
    c_buf,
    ct_buf,
    e_all,
    tot_buf,
    tot_in1,
    tot_mid,
    tot_in2,
    rc_buf,
    cp_buf,
    ts_buf,
    rs1_in,
    rs2_out,
    rs2_in,
    rs3_out,
    rs3_in,
    s1_send,
    s1_recv,
    s2_send,
    s2_recv,
    s3_send,
    s3_recv,
    code_send,
    code_recv,
    code_local,
    t1_send,
    t1_recv,
    t2_send,
    t2_recv,
    r1_send,
    r1_recv,
    r2_send,
    r2_recv,
    r3_send,
    r3_recv,
):
    n_dp, n_proto, n_crop, images, crops, tile = sizes
    n_plane, n_z = n_dp * n_crop, n_proto // 2
    shard = images * crops
    unit = n_z * shard
    group = n_proto * images
    owned = proto_ref.shape[0]
    tiles = owned // tile

    my_dp, my_proto, my_crop = (lax.axis_index(a) for a in ("dp", "proto", "crop"))
    plane = my_dp * n_crop + my_crop
    zi, core = my_proto // 2, my_proto % 2
    sibling = {"proto": zi * 2 + (1 - core)}

    def plane_peer(d):
        q = lax.rem(plane + d, n_plane)
        return q, {"dp": q // n_crop, "crop": q % n_crop}

    def plane_from(d):
        return lax.rem(plane + n_plane - d, n_plane)

    def z_peer(d):
        other = lax.rem(zi + d, n_z)
        return other, {"proto": other * 2 + core}

    def proto_peer(d):
        return {"proto": lax.rem(my_proto + d, n_proto)}

    def remote(src, dst, send, recv, device):
        return pltpu.make_async_remote_copy(
            src_ref=src, dst_ref=dst, send_sem=send, recv_sem=recv,
            device_id=device, device_id_type=MESH,
        )

    barrier = pltpu.get_barrier_semaphore()
    for d in range(1, n_proto):
        pl.semaphore_signal(barrier, inc=1, device_id=proto_peer(d), device_id_type=MESH)
    for d in range(1, n_plane):
        pl.semaphore_signal(barrier, inc=1, device_id=plane_peer(d)[1], device_id_type=MESH)

    own_codes = pltpu.make_async_copy(
        codes_ref.at[:, pl.ds(pl.multiple_of(plane * owned, owned), owned)],
        c_all.at[pl.ds(pl.multiple_of(plane * group, group), group), :],
        code_local,
    )
    own_codes.start()
    emb_floats = emb_ref[...].astype(jnp.float32)
    emb_rows = jnp.concatenate([emb_floats[:, v, :] for v in range(crops)], axis=0)
    unit_e, emb_length = unit_rows(emb_rows)
    own_rows = pl.ds(pl.multiple_of(zi * shard, shard), shard)
    z_all[core, plane, own_rows, :] = unit_e.astype(jnp.bfloat16)

    pl.semaphore_wait(barrier, n_proto - 1 + n_plane - 1)

    sent = []
    s1 = []
    for d in range(1, n_z):
        ref = z_all.at[core, plane, own_rows, :]
        s1.append(remote(ref, ref, s1_send.at[d - 1], s1_recv.at[d - 1], z_peer(d)[1]))
        s1[-1].start()

    s2 = {}

    def send_shard(dz):
        source = lax.rem(zi + n_z - dz, n_z)
        ref = z_all.at[core, plane, pl.ds(pl.multiple_of(source * shard, shard), shard), :]
        for d in range(1, n_plane):
            sem = dz * (n_plane - 1) + d - 1
            s2[dz, d] = remote(ref, ref, s2_send.at[sem], s2_recv.at[sem], plane_peer(d)[1])
            s2[dz, d].start()

    send_shard(0)
    code_copies = []
    for d in range(1, n_plane):
        q, device = plane_peer(d)
        code_copies.append(remote(
            codes_ref.at[:, pl.ds(pl.multiple_of(q * owned, owned), owned)],
            c_all.at[pl.ds(pl.multiple_of(plane * group, group), group), :],
            code_send.at[d - 1], code_recv.at[d - 1], device,
        ))
        code_copies[-1].start()
    sent += code_copies

    def tile_rows(t):
        return pl.ds(pl.multiple_of(t * tile, tile), tile)

    def normalize_tile(t, carry):
        unit_w = unit_rows(proto_ref[tile_rows(t), :])[0]
        c_buf[tile_rows(t), :] = unit_w.astype(jnp.bfloat16)
        ct_buf[:, tile_rows(t)] = unit_w.T.astype(jnp.bfloat16)
        return carry

    lax.fori_loop(0, tiles, normalize_tile, 0, unroll=True)

    for dz in range(1, n_z):
        s1[dz - 1].wait_recv()
        send_shard(dz)
    def score_unit(half, q):
        rows = z_all[half, q]

        def score_tile(t, sums):
            scores = lax.dot_general(
                c_buf[tile_rows(t), :], rows, (((1,), (1,)), ((), ())),
                preferred_element_type=jnp.float32,
            )
            exponent = jnp.exp(scores * sharpness)
            e_all[half * n_plane + q, tile_rows(t), :] = exponent.astype(jnp.bfloat16)
            return sums + jnp.sum(exponent, axis=0, keepdims=True)

        sums = lax.fori_loop(
            0, tiles, score_tile, jnp.zeros((1, unit), jnp.float32), unroll=True
        )
        tot_buf[pl.ds(half * n_plane + q, 1), :] = sums

    def soften_unit(u):
        columns = jnp.dot(ct_buf[...], e_all[u], preferred_element_type=jnp.float32)
        rc_buf[u] = columns.T

    s3 = []
    for d in range(n_plane):
        q = plane_from(d)
        for dz in range(n_z if d else 0):
            s2[dz, d].wait_recv()
        ref = z_all.at[core, q]
        s3.append(remote(ref, ref, s3_send.at[d], s3_recv.at[d], sibling))
        s3[-1].start()
        score_unit(core, q)
        soften_unit(core * n_plane + q)
    for d in range(n_plane):
        s3[d].wait_recv()
        score_unit(1 - core, plane_from(d))

    t1 = []
    for d in range(1, n_proto):
        t1.append(remote(
            tot_buf, tot_in1.at[d - 1], t1_send.at[d - 1], t1_recv.at[d - 1], proto_peer(d)
        ))
        t1[-1].start()

    for d in range(n_plane):
        soften_unit((1 - core) * n_plane + plane_from(d))

    total = tot_buf[...]
    for d in range(1, n_proto):
        t1[d - 1].wait_recv()
        total = total + tot_in1[d - 1]
    tot_mid[...] = total
    t2 = []
    for d in range(1, n_plane):
        t2.append(remote(
            tot_mid, tot_in2.at[d - 1], t2_send.at[d - 1], t2_recv.at[d - 1], plane_peer(d)[1]
        ))
        t2[-1].start()
    sent += t2

    def image_rows(half, z):
        return pl.ds((z * 2 + half) * images, images)

    def crop_rows(z, v):
        return pl.ds(z * shard + v * images, images)

    def target_group(a, carry):
        for half in range(2):
            for z in range(n_z):
                locals_sum = None
                for g in range(n_crop):
                    for v in range(1, crops):
                        term = z_all[half, a * n_crop + g, crop_rows(z, v), :].astype(jnp.float32)
                        locals_sum = term if locals_sum is None else locals_sum + term
                for t in range(n_crop):
                    other = z_all[half, a * n_crop + 1 - t, crop_rows(z, 0), :]
                    ts_buf[a, t, image_rows(half, z), :] = (
                        locals_sum + other.astype(jnp.float32)
                    ).astype(jnp.bfloat16)
        return carry

    lax.fori_loop(0, n_dp, target_group, 0)

    own_codes.wait()
    for copy in code_copies:
        copy.wait_recv()

    code_rows = n_plane * group
    chunk = min(code_rows, 512)

    def code_products(k, carry):
        rows = pl.ds(pl.multiple_of(k * chunk, chunk), chunk)
        cp_buf[rows, :] = jnp.dot(
            c_all[rows, :], c_buf[...], preferred_element_type=jnp.float32
        )
        return carry

    lax.fori_loop(0, code_rows // chunk, code_products, 0)

    total = tot_mid[...]
    for d in range(1, n_plane):
        t2[d - 1].wait_recv()
        total = total + tot_in2[d - 1]
    crop_of = lax.rem(lax.broadcasted_iota(jnp.int32, total.shape, 1) // images, crops)
    tot_buf_weights = jnp.where(crop_of == 0, 1.0, 2.0) / total
    for copy in t1 + s1 + list(s2.values()) + s3:
        copy.wait_send()
    tot_buf[...] = tot_buf_weights

    lanes = 128

    def row_unit(half, q):
        u = half * n_plane + q
        weights = tot_buf[pl.ds(u, 1), :]
        a, g = q // n_crop, q % n_crop
        for b in range(unit // lanes):
            part = pl.ds(b * lanes, lanes)
            column = jnp.broadcast_to(weights[:, b * lanes:(b + 1) * lanes], (lanes, lanes)).T
            column = jnp.concatenate([column] * (z_all.shape[-1] // lanes), axis=1)
            z_all[half, q, part, :] = (
                z_all[half, q, part, :].astype(jnp.float32) * column
            ).astype(jnp.bfloat16)
            rc_buf[u, part, :] = rc_buf[u, part, :] * column
        for z in range(n_z):
            def code_part(t):
                start = (a * n_crop + t) * group + (z * 2 + half) * images
                return cp_buf[pl.ds(pl.multiple_of(start, images), images), :]

            other = code_part(1 - g)
            both = other + code_part(g)
            for v in range(crops):
                code_term = other if v == 0 else both
                rc_buf[u, crop_rows(z, v), :] = (
                    rc_buf[u, crop_rows(z, v), :] - code_term
                ) * sharpness

    r1 = {}
    order = list(range(1, n_plane)) + [0]
    for d in order:
        q = plane_from(d)
        row_unit(1 - core, q)
        r1[d] = remote(
            rc_buf.at[(1 - core) * n_plane + q], rs1_in.at[q],
            r1_send.at[d], r1_recv.at[d], sibling,
        )
        r1[d].start()
    sent += list(r1.values())

    r2 = []
    for d in order:
        q = plane_from(d)
        row_unit(core, q)
        r1[d].wait_recv()
        if d == 0:
            continue
        rs2_out[d - 1] = (rc_buf[core * n_plane + q] + rs1_in[q]).astype(jnp.bfloat16)
        device = {"dp": q // n_crop, "crop": q % n_crop}
        r2.append(remote(
            rs2_out.at[d - 1], rs2_in.at[d - 1], r2_send.at[d - 1], r2_recv.at[d - 1], device
        ))
        r2[-1].start()
    sent += r2

    wide = min(owned, 2 * tile)

    def out_copy(t):
        rows = pl.ds(pl.multiple_of(t * wide, wide), wide)
        return pltpu.make_async_copy(gp_buf.at[rows, :], gproto_ref.at[rows, :], gp_sem.at[t])

    def proto_tile(t, carry):
        rows = pl.ds(pl.multiple_of(t * wide, wide), wide)
        exponents = jnp.concatenate([e_all[u, rows, :] for u in range(2 * n_plane)], axis=1)
        weighted = z_all[...].reshape(2 * n_plane * unit, z_all.shape[-1])
        grad = jnp.dot(exponents, weighted, preferred_element_type=jnp.float32)
        targets = ts_buf[...].reshape(n_plane * group, ts_buf.shape[-1])
        grad = grad - lax.dot_general(
            c_all[:, rows], targets, (((0,), (0,)), ((), ())), preferred_element_type=jnp.float32
        )
        unit_w, length = unit_rows(proto_ref[rows, :])
        along = jnp.sum(unit_w * grad, axis=-1, keepdims=True)
        gp_buf[rows, :] = (grad - unit_w * along) / length
        out_copy(t).start()
        return carry

    first = (owned // wide) * 3 // 4
    lax.fori_loop(0, first, proto_tile, 0)

    rows_sum = rc_buf[core * n_plane + plane] + rs1_in[plane]
    for copy in r2:
        copy.wait_recv()
    for d in range(1, n_plane):
        rows_sum = rows_sum + rs2_in[d - 1].astype(jnp.float32)
    rs3_out[...] = rows_sum
    r3 = []
    for d in range(1, n_z):
        other, device = z_peer(d)
        r3.append(remote(
            rs3_out.at[pl.ds(pl.multiple_of(other * shard, shard), shard), :], rs3_in.at[d - 1],
            r3_send.at[d - 1], r3_recv.at[d - 1], device,
        ))
        r3[-1].start()
    sent += r3

    lax.fori_loop(first, owned // wide, proto_tile, 0)

    score_grad = rs3_out[own_rows, :]
    for d in range(1, n_z):
        r3[d - 1].wait_recv()
        score_grad = score_grad + rs3_in[d - 1]
    along = jnp.sum(unit_e * score_grad, axis=-1, keepdims=True)
    grad_rows = (score_grad - unit_e * along) / emb_length
    for v in range(crops):
        gemb_ref[:, v, :] = grad_rows[v * images:(v + 1) * images]
    for t in range(owned // wide):
        out_copy(t).wait()
    for copy in sent:
        copy.wait_send()


def on_device(sizes, embeddings, codes, prototypes):
    n_dp, n_proto, n_crop = sizes
    images, _, crops, features = embeddings.shape
    owned = prototypes.shape[1]
    n_plane, n_z = n_dp * n_crop, n_proto // 2
    shard = images * crops
    unit = n_z * shard
    group = codes.shape[0]
    units = 2 * n_plane
    tile = min(owned, 256)
    vmem = pl.BlockSpec(memory_space=pltpu.VMEM)
    dma = pltpu.SemaphoreType.DMA
    bf16, f32 = jnp.bfloat16, jnp.float32
    pairs = [n_z - 1, n_z * (n_plane - 1), n_plane, n_plane - 1]
    sems = []
    for count in pairs:
        sems += [dma((max(count, 1),)), dma((max(count, 1),))]
    sems.append(dma)
    for count in (n_proto - 1, n_plane - 1, n_plane, n_plane - 1, n_z - 1):
        sems += [dma((max(count, 1),)), dma((max(count, 1),))]
    scratch = [
        pltpu.VMEM((owned, features), f32),
        dma((max(owned // (2 * tile), 1),)),
        pltpu.VMEM((2, n_plane, unit, features), bf16),
        pltpu.VMEM((n_plane * group, owned), bf16),
        pltpu.VMEM((owned, features), bf16),
        pltpu.VMEM((features, owned), bf16),
        pltpu.VMEM((units, owned, unit), bf16),
        pltpu.VMEM((units, unit), f32),
        pltpu.VMEM((n_proto - 1, units, unit), f32),
        pltpu.VMEM((units, unit), f32),
        pltpu.VMEM((max(n_plane - 1, 1), units, unit), f32),
        pltpu.VMEM((units, unit, features), f32),
        pltpu.VMEM((n_plane * group, features), f32),
        pltpu.VMEM((n_dp, n_crop, group, features), bf16),
        pltpu.VMEM((n_plane, unit, features), f32),
        pltpu.VMEM((max(n_plane - 1, 1), unit, features), bf16),
        pltpu.VMEM((max(n_plane - 1, 1), unit, features), bf16),
        pltpu.VMEM((unit, features), f32),
        pltpu.VMEM((max(n_z - 1, 1), shard, features), f32),
    ]
    held = sum(math.prod(x.shape) * jnp.dtype(x.dtype).itemsize for x in [scratch[0]] + scratch[2:])
    grant = min(62 * 2**20, held * 5 // 4 + 8 * 2**20)
    grad_emb, grad_proto = pl.pallas_call(
        functools.partial(kernel, (n_dp, n_proto, n_crop, images, crops, tile)),
        out_shape=(
            jax.ShapeDtypeStruct((images, crops, features), f32),
            jax.ShapeDtypeStruct((owned, features), f32),
        ),
        in_specs=[vmem, pl.BlockSpec(memory_space=pl.ANY), vmem],
        out_specs=(vmem, pl.BlockSpec(memory_space=pl.ANY)),
        scratch_shapes=scratch + sems,
        compiler_params=pltpu.CompilerParams(
            collective_id=0, has_side_effects=True, vmem_limit_bytes=grant
        ),
        cost_estimate=pl.CostEstimate(
            flops=6 * units * unit * owned * features, bytes_accessed=8 * owned * features,
            transcendentals=units * unit * owned,
        ),
    )(embeddings[:, 0], codes[:, 0], prototypes[0])
    return grad_emb[:, None], grad_proto[None]


def solution(mesh):
    sizes = tuple(mesh.shape[a] for a in ("dp", "proto", "crop"))
    return jax.shard_map(
        functools.partial(on_device, sizes),
        mesh=mesh,
        in_specs=(
            P(("dp", "proto"), "crop", None, None),
            P("dp", "crop", "proto"),
            P("proto", ("dp", "crop"), None),
        ),
        out_specs=(P(("dp", "proto"), "crop", None, None), P("proto", ("dp", "crop"), None)),
        check_vma=False,
    )
```
